32 devices in a mesh: gx: 4 (over x, core), gy: 8 (over z, y).
Axes of the slice: x: 2, y: 2, z: 4, core: 2. Of those that a mesh axis runs over, the one named last changes fastest.
Arguments:
- fields: float32 [6, 64, 256, 128], P(None, 'gx', 'gy'), may hold values from -6 to 6
- material: int32 [64, 256, 128], P('gx', 'gy'), may hold values from 0 to 15
- ca_table: float32 [16], replicated, may hold values from 0.6 to 1
- cb_table: float32 [16], replicated, may hold values from 0.2 to 0.5
- fine: float32 [4, 8, 8, 2, 128], P('gx', 'gy'), may hold values from -6 to 6
- face_target: int32 [4, 8, 8, 2], P('gx', 'gy'), may hold values from -1 to 511, as said below
- surf_start: int32 [4, 8], P('gx', 'gy'), may hold values from 0 to 24
- surf_count: int32 [4, 8], P('gx', 'gy'), may hold values from 0 to 8, as said below
- omega: float32 [32], replicated, may hold values from 0.3 to 2.5
- bearing: float32 [4096], replicated, may hold values from -3.140625 to 3.140625
Outputs:
- fields_out: float32 [6, 64, 256, 128], P(None, 'gx', 'gy')
- fine_out: float32 [4, 8, 8, 2, 128], P('gx', 'gy')
- far_field: float32 [4, 2, 32, 4096], P('gx')
The draws below stay inside these ranges and needn't reach their ends.
Inputs may be any that keep to these rules, and one draw needn't show every extreme that they name: `face_target`: live cells of one owner within a gx row are distinct; in each gx row some owner has all 2 slots from every device live. `surf_count`: some device has exactly 8 rows.
All inputs are finite; a program needn't handle non-finite values.
Results may differ from the reference program's by a relative error of at most 0.00017.
Values sent between devices are 32-bit elements; how exact they have to be, the bound alone decides.
A program may use at most 64 MiB of HBM per device.

```python
import math
import jax
import jax.numpy as jnp
from jax import lax

CX = 16
CY = 32
NZ = 128
STEPS = 4
F = 32
A = 4096
SY = 8
CAP = 2
M = 16
NX = 64
NY = 256
N_GX = 4
N_GY = 8


def face_tables(key):
    key_order, key_live, key_full = jax.random.split(key, 3)
    cells = CX * CY
    scores = jax.random.randint(key_order, (N_GX, N_GY, cells), 0, 2 ** 20) * cells + jnp.arange(cells, dtype=jnp.int32)
    order = jnp.argsort(scores, axis=-1, stable=True)[..., :N_GY * CAP].reshape(N_GX, N_GY, N_GY, CAP)
    live = jax.random.randint(key_live, (N_GX, N_GY, N_GY, CAP), 0, 5) < 3
    full = jax.random.randint(key_full, (N_GX,), 0, N_GY)
    live = live | (jnp.arange(N_GY)[None, :, None, None] == full[:, None, None, None])
    return jnp.where(live, order, -1).astype(jnp.int32)


def draw_face_target(key, part):
    return face_tables(key)


def draw_surf_count(key, part):
    key = jax.random.fold_in(key, 7)
    key_count, key_place = jax.random.split(key)
    counts = jax.random.randint(key_count, (N_GX * N_GY,), 0, SY + 1)
    place = jax.random.randint(key_place, (), 0, N_GX * N_GY)
    counts = counts.at[place].set(SY)
    return counts.reshape(N_GX, N_GY).astype(jnp.int32)


def with_ends(array, own_key, smallest, high):
    longest = array.shape.index(max(array.shape))
    spots = []
    for shift in (0, 1):
        where = [jax.random.randint(jax.random.fold_in(own_key, axis), (), 0, length) for axis, length in enumerate(array.shape)]
        where[longest] = (where[longest] + shift) % array.shape[longest]
        spots.append(tuple(where))
    return array.at[spots[0]].set(smallest).at[spots[1]].set(high)


def level_of(own_key, dims, shards, least, top_value):
    def one(dim, shards_of):
        steps = jax.random.uniform(jax.random.fold_in(jax.random.fold_in(own_key, 6), dim), (shards_of,), jnp.float32, least / len(shards), top_value / len(shards))
        return jnp.repeat(jnp.exp(steps), dims[dim] // shards_of).reshape((-1,) + (1,) * (len(dims) - dim - 1))

    level = one(*shards[0])
    for cut in shards[1:]:
        level = level * one(*cut)
    return level


def noise(own_key, extent, scale, limit, shards=(), kind=jnp.bfloat16):
    values = scale * jax.random.normal(own_key, extent, jnp.float32)
    if shards:
        values = values * level_of(own_key, extent, shards, -0.22, 0.18)
    return jnp.clip(values, -limit, limit).astype(kind)


def setup_inputs(seed: int = 0) -> dict:
    key_of = jax.random.split(jax.random.key(seed), 11)
    return {
        "fields": noise(key_of[0], (6, NX, NY, NZ), 1.0, 6.0, ((1, 4), (2, 8)), jnp.float32),
        "material": with_ends(jax.random.randint(key_of[1], (NX, NY, NZ), 0, M), jax.random.fold_in(key_of[1], 1), 0, M - 1).astype(jnp.int32),
        "ca_table": jnp.clip(jax.random.uniform(key_of[2], (M,), jnp.float32, 0.6, 1.0), 0.6, 1.0),
        "cb_table": jnp.clip(jax.random.uniform(key_of[3], (M,), jnp.float32, 0.2, 0.5), 0.2, 0.5),
        "fine": noise(key_of[4], (N_GX, N_GY, N_GY, CAP, NZ), 1.0, 6.0, ((0, 4), (1, 8)), jnp.float32),
        "face_target": draw_face_target(jax.random.fold_in(key_of[10], 71), 0),
        "surf_start": with_ends(jax.random.randint(key_of[6], (N_GX, N_GY), 0, CY - SY + 1), jax.random.fold_in(key_of[6], 1), 0, CY - SY).astype(jnp.int32),
        "surf_count": draw_surf_count(jax.random.fold_in(key_of[10], 71), 0),
        "omega": jnp.clip(jnp.exp(jax.random.uniform(key_of[8], (F,), jnp.float32, math.log(0.3), math.log(2.5))), 0.3, 2.5),
        "bearing": jnp.clip(jax.random.uniform(key_of[9], (A,), jnp.float32, -3.140625, 3.140625), -3.140625, 3.140625),
    }


DTH = 0.5
KAPPA = 0.25
WAVENUM = 0.35

def step_ahead(value, axis):
    count = value.shape[axis]
    rest = lax.slice_in_dim(value, 1, count, axis=axis)
    return jnp.concatenate([rest, jnp.zeros_like(lax.slice_in_dim(value, 0, 1, axis=axis))], axis)

def step_behind(value, axis):
    count = value.shape[axis]
    rest = lax.slice_in_dim(value, 0, count - 1, axis=axis)
    return jnp.concatenate([jnp.zeros_like(lax.slice_in_dim(value, 0, 1, axis=axis)), rest], axis)

def far_part(j_real, j_imag, ypos, bearing):
    zpos = jnp.arange(j_real.shape[-1]).astype(jnp.float32)
    cos_z = jnp.cos(WAVENUM * zpos[:, None] * jnp.cos(bearing)[None, :])
    sin_z = jnp.sin(WAVENUM * zpos[:, None] * jnp.cos(bearing)[None, :])
    cos_y = jnp.cos(WAVENUM * ypos[:, None] * jnp.sin(bearing)[None, :])
    sin_y = jnp.sin(WAVENUM * ypos[:, None] * jnp.sin(bearing)[None, :])
    high = lax.Precision.HIGHEST
    q_real = jnp.einsum('frz,za->fra', j_real, cos_z, precision=high) - jnp.einsum('frz,za->fra', j_imag, sin_z, precision=high)
    q_imag = jnp.einsum('frz,za->fra', j_real, sin_z, precision=high) + jnp.einsum('frz,za->fra', j_imag, cos_z, precision=high)
    p_real = lax.optimization_barrier(jnp.sum(q_real * cos_y[None] - q_imag * sin_y[None], axis=1))
    p_imag = lax.optimization_barrier(jnp.sum(q_real * sin_y[None] + q_imag * cos_y[None], axis=1))
    return jnp.stack([p_real, p_imag])

def reference(fields, material, ca_table, cb_table, fine, face_target, surf_start, surf_count, omega, bearing):
    ca_cell = ca_table[material]
    cb_cell = cb_table[material]
    efield_x, efield_y, efield_z = (fields[0], fields[1], fields[2])
    hfield_x, hfield_y, hfield_z = (fields[3], fields[4], fields[5])
    live = face_target >= 0
    cell = jnp.where(live, face_target, 0)
    grow = jnp.arange(N_GX)[:, None, None, None]
    orow = jnp.arange(N_GY)[None, :, None, None]
    xs_idx = (grow * CX + cell // CY).astype(jnp.int32)
    ys_idx = (orow * CY + cell % CY).astype(jnp.int32)
    fine_own = jnp.transpose(fine, (0, 2, 1, 3, 4))
    rows = jnp.arange(SY)
    dev_idx = jnp.arange(N_GY)
    yidx = (dev_idx[None, :, None] * CY + surf_start[:, :, None] + rows[None, None, :]).astype(jnp.int32)
    row_mask = (rows[None, None, :] < surf_count[:, :, None]).astype(jnp.float32)
    gsel = jnp.arange(N_GX)[:, None, None]
    j_real = jnp.zeros((N_GX, N_GY, F, SY, NZ), jnp.float32)
    j_imag = jnp.zeros((N_GX, N_GY, F, SY, NZ), jnp.float32)
    for tick in range(STEPS):
        curl_x = step_ahead(efield_z, 1) - efield_z - (step_ahead(efield_y, 2) - efield_y)
        curl_y = step_ahead(efield_x, 2) - efield_x - (step_ahead(efield_z, 0) - efield_z)
        curl_z = step_ahead(efield_y, 0) - efield_y - (step_ahead(efield_x, 1) - efield_x)
        hfield_x = hfield_x - DTH * curl_x
        hfield_y = hfield_y - DTH * curl_y
        hfield_z = hfield_z - DTH * curl_z
        curl_x = hfield_z - step_behind(hfield_z, 1) - (hfield_y - step_behind(hfield_y, 2))
        curl_y = hfield_x - step_behind(hfield_x, 2) - (hfield_z - step_behind(hfield_z, 0))
        curl_z = hfield_y - step_behind(hfield_y, 0) - (hfield_x - step_behind(hfield_x, 1))
        efield_x = ca_cell * efield_x + cb_cell * curl_x
        efield_y = ca_cell * efield_y + cb_cell * curl_y
        efield_z = ca_cell * efield_z + cb_cell * curl_z
        line = efield_z[xs_idx, ys_idx]
        added = jnp.where(live[..., None], KAPPA * (fine_own - line), jnp.float32(0.0))
        efield_z = efield_z.at[xs_idx, ys_idx].add(added)
        back = efield_z[xs_idx, ys_idx]
        fine_own = jnp.where(live[..., None], fine_own + 0.5 * (back - fine_own), fine_own)
        plane = efield_z[::CX] + hfield_y[::CX]
        window = plane[gsel, yidx] * row_mask[..., None]
        moment = omega * jnp.float32(tick + 1)
        j_real = j_real + jnp.cos(moment)[None, None, :, None, None] * window[:, :, None]
        j_imag = j_imag - jnp.sin(moment)[None, None, :, None, None] * window[:, :, None]
    ypos = yidx.astype(jnp.float32)

    def per_row(gnum):

        def add_device(total, dnum):
            return (total + far_part(j_real[gnum, dnum], j_imag[gnum, dnum], ypos[gnum, dnum], bearing), None)
        total, unused = lax.scan(add_device, jnp.zeros((2, F, A), jnp.float32), jnp.arange(N_GY))
        return total
    norm = 1.0 / math.sqrt(N_GY * SY * NZ)
    far_field = lax.map(per_row, jnp.arange(N_GX)) * norm
    fields_out = jnp.stack([efield_x, efield_y, efield_z, hfield_x, hfield_y, hfield_z])
    fine_out = jnp.transpose(fine_own, (0, 2, 1, 3, 4))
    return (fields_out, fine_out, far_field)
```

```python
import functools
import math

import jax
import jax.numpy as jnp
from jax import lax
from jax.experimental import pallas as pl
from jax.experimental.pallas import tpu as pltpu
from jax.sharding import PartitionSpec as P

STEPS = 4
SY = 8
DTH = 0.5
KAPPA = 0.25
WAVENUM = 0.35
PAD = 8

MESH = pl.DeviceIdType.MESH
HIGH = lax.Precision.HIGHEST


def iota(shape, dim):
    return lax.broadcasted_iota(jnp.int32, shape, dim)


def rows_up(value, last):
    count = value.shape[0]
    return jnp.where(iota(value.shape, 0) == count - 1, last, pltpu.roll(value, count - 1, 0))


def z_up(value):
    count = value.shape[1]
    return jnp.where(iota(value.shape, 1) == count - 1, 0.0, pltpu.roll(value, count - 1, 1))


def z_down(value):
    return jnp.where(iota(value.shape, 1) == 0, 0.0, pltpu.roll(value, 1, 1))


def kernel(
    n_x, n_y,
    fields, material, fine, bearing, ca_table, cb_table, target, start, count, omega,
    fields_out, fine_out, far_out,
    e_buf, h_buf, ca_buf, cb_buf, fd_buf, mk_buf, mat,
    xt, xh, yt, yh, c1, c2, gx_in, gy_in,
    syt, syh, sgy, sc1, sc2,
    s_all, fin, fpad, fback, fhome, table, yc, ys, w_buf, g_all, far_buf,
    load_sem, send_sem, recv_sem, s_send, s_recv, f_send, f_recv, g_send, g_recv, out_sem,
):
    _, cx, cy, nz = fields.shape
    slots = fine.shape[1]
    local_a = g_all.shape[2]
    freqs = omega.shape[0]
    gx = lax.axis_index("gx")
    gy = lax.axis_index("gy")
    has_l, has_r = gx > 0, gx < n_x - 1
    has_d, has_u = gy > 0, gy < n_y - 1
    left, right = (gx - 1, gy), (gx + 1, gy)
    down, up = (gx, gy - 1), (gx, gy + 1)
    left_up, right_down = (gx - 1, gy + 1), (gx + 1, gy - 1)
    has_lu, has_rd = has_l & has_u, has_r & has_d

    loads = [
        pltpu.make_async_copy(fields.at[0:3], e_buf.at[:, 0:cx, 0:cy], load_sem.at[0]),
        pltpu.make_async_copy(fields.at[3:6], h_buf.at[:, 1 : cx + 1, PAD : PAD + cy], load_sem.at[1]),
        pltpu.make_async_copy(material, mat, load_sem.at[2]),
        pltpu.make_async_copy(fine.at[gy], fin.at[gy], load_sem.at[3]),
    ]
    for load in loads:
        load.start()

    barrier = pltpu.get_barrier_semaphore()
    for has, where in ((has_l, left), (has_r, right), (has_lu, left_up), (has_rd, right_down)):

        @pl.when(has)
        def _(where=where):
            pl.semaphore_signal(barrier, inc=1, device_id=where, device_id_type=MESH)

    def peer_of(k):
        return lax.rem(gy + k, n_y)

    def greet(k, carry):
        pl.semaphore_signal(barrier, inc=1, device_id=(gx, peer_of(k)), device_id_type=MESH)
        return carry

    lax.fori_loop(1, n_y, greet, 0)

    for has, refs in (
        (has_l, (xt, gx_in)), (has_r, (xh,)), (has_d, (yt, gy_in)), (has_u, (yh,)), (has_lu, (c1,)), (has_rd, (c2,)),
    ):

        @pl.when(jnp.logical_not(has))
        def _(refs=refs):
            for ref in refs:
                ref[...] = jnp.zeros(ref.shape, ref.dtype)

    s_all[STEPS, gy] = jnp.broadcast_to(start[0, 0].astype(jnp.float32), (SY, nz))
    arrivals = (
        has_l.astype(jnp.int32) + has_r.astype(jnp.int32) + has_lu.astype(jnp.int32) + has_rd.astype(jnp.int32)
    )
    pl.semaphore_wait(barrier, arrivals + (n_y - 1))

    def remote(index, src, dst, where):
        return pltpu.make_async_remote_copy(
            src_ref=src, dst_ref=dst, send_sem=send_sem.at[index], recv_sem=recv_sem.at[index],
            device_id=where, device_id_type=MESH,
        )

    def x_copies(t, src_tail, src_head):
        return [
            (has_r, has_l, remote(6 * t + 0, src_tail, xt.at[t], right)),
            (has_l, has_r, remote(6 * t + 1, src_head, xh.at[t], left)),
        ]

    def y_copies(t):
        return [
            (has_u, has_d, remote(6 * t + 2, syt.at[t], yt.at[t], up)),
            (has_d, has_u, remote(6 * t + 3, syh.at[t], yh.at[t], down)),
            (has_rd, has_lu, remote(6 * t + 4, sc1.at[t], c1.at[t], right_down)),
            (has_lu, has_rd, remote(6 * t + 5, sc2.at[t], c2.at[t], left_up)),
        ]

    def begin(copies):
        for sends, _, copy in copies:

            @pl.when(sends)
            def _(copy=copy):
                copy.start()

    def arrived(copies):
        for _, comes, copy in copies:

            @pl.when(comes)
            def _(copy=copy):
                copy.wait_recv()

    def sent(copies):
        for sends, _, copy in copies:

            @pl.when(sends)
            def _(copy=copy):
                copy.wait_send()

    def to_peers(src_of, dst, sends, recvs):
        def one(k, carry):
            peer = peer_of(k)
            pltpu.make_async_remote_copy(
                src_ref=src_of(peer), dst_ref=dst, send_sem=sends, recv_sem=recvs,
                device_id=(gx, peer), device_id_type=MESH,
            ).start()
            return carry

        lax.fori_loop(1, n_y, one, 0)

    def wait_all(ref, sem):
        part = ref.at[0 : n_y - 1]
        pltpu.make_async_copy(part, part, sem).wait()

    x_now = x_copies(0, fields.at[0:3, cx - 1], fields.at[1:3, 0])
    x_now.append((has_r, has_l, remote(6 * STEPS, fields.at[4:6, cx - 1], gx_in, right)))
    begin(x_now)
    to_peers(lambda peer: fine.at[peer], fin.at[gy], f_send.at[0], f_recv.at[0])
    to_peers(lambda peer: s_all.at[STEPS, gy], s_all.at[STEPS, gy], s_send.at[STEPS], s_recv.at[STEPS])

    for load in loads[:2]:
        load.wait()

    def stage(x, carry):
        for comp in range(3):
            syt[0, comp, pl.ds(x, 1), :] = e_buf[comp, x, cy - 1 : cy, :]
        syh[0, 0, pl.ds(x, 1), :] = e_buf[0, x, 0:1, :]
        syh[0, 1, pl.ds(x, 1), :] = e_buf[2, x, 0:1, :]
        sgy[0, pl.ds(x, 1), :] = h_buf[0, x + 1, PAD + cy - 1 : PAD + cy, :]
        sgy[1, pl.ds(x, 1), :] = h_buf[2, x + 1, PAD + cy - 1 : PAD + cy, :]
        return carry

    lax.fori_loop(0, cx, stage, 0)

    def stage_corners(t):
        sc1[t] = jnp.broadcast_to(e_buf[0, cx - 1, 0:1, :], (8, nz))
        sc2[t] = jnp.broadcast_to(e_buf[1, 0, cy - 1 : cy, :], (8, nz))

    stage_corners(0)
    y_now = y_copies(0)
    y_now.append((has_u, has_d, remote(6 * STEPS + 1, sgy, gy_in, up)))
    begin(y_now)

    for load in loads[2:]:
        load.wait()

    def look_up(x, carry):
        index = mat[x]
        ca = jnp.zeros((cy, nz), jnp.float32)
        cb = jnp.zeros((cy, nz), jnp.float32)
        for m in range(ca_table.shape[0]):
            chosen = index == m
            ca = jnp.where(chosen, ca_table[m], ca)
            cb = jnp.where(chosen, cb_table[m], cb)
        ca_buf[x] = ca
        cb_buf[x] = cb
        return carry

    lax.fori_loop(0, cx, look_up, 0)

    angle = bearing[:, pl.ds(pl.multiple_of(gy * local_a, local_a), local_a)]
    cos_b, sin_b = jnp.cos(angle), jnp.sin(angle)
    arg_low = (WAVENUM * iota((8, local_a), 0).astype(jnp.float32)) * cos_b
    cos_low, sin_low = jnp.cos(arg_low), jnp.sin(arg_low)
    tops = nz // 8
    arg_top = ((WAVENUM * 8) * iota((tops, local_a), 0).astype(jnp.float32)) * cos_b
    cos_top, sin_top = jnp.cos(arg_top), jnp.sin(arg_top)
    for top in range(tops):
        ct, st = cos_top[top : top + 1], sin_top[top : top + 1]
        table[8 * top : 8 * top + 8, 0:local_a] = ct * cos_low - st * sin_low
        table[8 * top : 8 * top + 8, local_a : 2 * local_a] = st * cos_low + ct * sin_low

    wait_all(fin, f_recv.at[0])
    fpad[...] = jnp.zeros(fpad.shape, jnp.float32)
    wide = fpad.shape[0]
    lane = iota((1, wide), 1)
    cell_row = jnp.full((1, wide), -1, jnp.int32)
    for holder in range(n_y):
        fpad[slots * holder : slots * (holder + 1), :] = fin[holder]
        for slot in range(slots):
            cell_row = jnp.where(lane == slots * holder + slot, target[holder, slot], cell_row)
    onehot = (iota((cx * cy, wide), 0) == cell_row).astype(jnp.float32).astype(jnp.bfloat16)
    rest = fpad[...]
    dense = jnp.zeros((cx * cy, nz), jnp.float32)
    for _ in range(3):
        part = rest.astype(jnp.bfloat16)
        rest = rest - part.astype(jnp.float32)
        dense = dense + jnp.dot(onehot, part, preferred_element_type=jnp.float32)
    fd_buf[...] = dense
    mk_buf[...] = jnp.dot(
        onehot, jnp.full((wide, nz), KAPPA, jnp.bfloat16), preferred_element_type=jnp.float32
    )

    om = jnp.zeros((freqs, 128), jnp.float32)
    for f in range(freqs):
        om = jnp.where(iota((freqs, 128), 0) == f, omega[f], om)
    lanes = iota((freqs, 128), 1)
    second = lanes >= STEPS
    tick_of = jnp.where(second, lanes - STEPS, lanes) + 1
    moment = om * tick_of.astype(jnp.float32)
    norm = 1.0 / math.sqrt(n_y * SY * nz)
    cos_m, sin_m = jnp.cos(moment) * norm, jnp.sin(moment) * norm
    w_buf[0:freqs, :] = jnp.where(second, sin_m, cos_m)
    w_buf[freqs : 2 * freqs, :] = jnp.where(second, cos_m, -sin_m)

    wait_all(s_all.at[STEPS], s_recv.at[STEPS])
    row_count = n_y * SY
    row = iota((row_count, nz), 0)
    spot = s_all[STEPS].reshape(row_count, nz) + ((row // SY) * cy + lax.rem(row, SY)).astype(jnp.float32)
    arg_y = (WAVENUM * spot[:, 0:1]) * sin_b
    yc[...] = jnp.cos(arg_y)
    ys[...] = jnp.sin(arg_y)

    keep_l = has_l.astype(jnp.float32)
    keep_d = has_d.astype(jnp.float32)
    row_mask = (iota((SY, nz), 0) < count[0, 0]).astype(jnp.float32)

    for t in range(STEPS):
        arrived(x_now)
        arrived(y_now)
        sent(x_now)
        if t == 0:
            h_buf[1, 0, PAD : PAD + cy, :] = gx_in[0]
            h_buf[2, 0, PAD : PAD + cy, :] = gx_in[1]
        ex, ey, ez = xt[t, 0], xt[t, 1], xt[t, 2]
        hy = h_buf[1, 0, PAD : PAD + cy, :]
        hz = h_buf[2, 0, PAD : PAD + cy, :]
        ahead = rows_up(ex, c1[t, 0:1, :])
        h_buf[1, 0, PAD : PAD + cy, :] = keep_l * (
            hy - DTH * ((z_up(ex) - ex) - (e_buf[2, 0, 0:cy, :] - ez))
        )
        h_buf[2, 0, PAD : PAD + cy, :] = keep_l * (
            hz - DTH * ((e_buf[1, 0, 0:cy, :] - ey) - (ahead - ex))
        )
        ex, ey, ez = yt[t, 0], yt[t, 1], yt[t, 2]
        ahead = rows_up(ey, c2[t, 0:1, :])
        gy_in[0] = keep_d * (gy_in[0] - DTH * ((syh[t, 1] - ez) - (z_up(ey) - ey)))
        gy_in[1] = keep_d * (gy_in[1] - DTH * ((ahead - ey) - (syh[t, 0] - ex)))
        e_buf[1, cx, 0:cy, :] = xh[t, 0]
        e_buf[2, cx, 0:cy, :] = xh[t, 1]

        def edges(x, carry, t=t):
            e_buf[0, x, cy : cy + 1, :] = yh[t, 0, pl.ds(x, 1), :]
            e_buf[2, x, cy : cy + 1, :] = yh[t, 1, pl.ds(x, 1), :]
            h_buf[0, x + 1, PAD - 1 : PAD, :] = gy_in[0, pl.ds(x, 1), :]
            h_buf[2, x + 1, PAD - 1 : PAD, :] = gy_in[1, pl.ds(x, 1), :]
            return carry

        lax.fori_loop(0, cx, edges, 0)

        def h_plane(x, carry):
            own = slice(PAD, PAD + cy)
            ex, ey, ez = (e_buf[comp, x, 0:cy, :] for comp in range(3))
            ex_y, ez_y = e_buf[0, x, 1 : cy + 1, :], e_buf[2, x, 1 : cy + 1, :]
            ey_x, ez_x = e_buf[1, x + 1, 0:cy, :], e_buf[2, x + 1, 0:cy, :]
            h_buf[0, x + 1, own, :] = h_buf[0, x + 1, own, :] - DTH * ((ez_y - ez) - (z_up(ey) - ey))
            h_buf[1, x + 1, own, :] = h_buf[1, x + 1, own, :] - DTH * ((z_up(ex) - ex) - (ez_x - ez))
            h_buf[2, x + 1, own, :] = h_buf[2, x + 1, own, :] - DTH * ((ey_x - ey) - (ex_y - ex))
            return carry

        lax.fori_loop(0, cx, h_plane, 0)

        def e_plane(x, carry, t=t):
            own = slice(PAD, PAD + cy)
            before = slice(PAD - 1, PAD + cy - 1)
            hx, hy, hz = (h_buf[comp, x + 1, own, :] for comp in range(3))
            hx_y, hz_y = h_buf[0, x + 1, before, :], h_buf[2, x + 1, before, :]
            hy_x, hz_x = h_buf[1, x, own, :], h_buf[2, x, own, :]
            ca, cb = ca_buf[x], cb_buf[x]
            ex = ca * e_buf[0, x, 0:cy, :] + cb * ((hz - hz_y) - (hy - z_down(hy)))
            ey = ca * e_buf[1, x, 0:cy, :] + cb * ((hx - z_down(hx)) - (hz - hz_x))
            ez = ca * e_buf[2, x, 0:cy, :] + cb * ((hy - hy_x) - (hx - hx_y))
            cells = pl.ds(pl.multiple_of(x * cy, cy), cy)
            mk, fd = mk_buf[cells, :], fd_buf[cells, :]
            ez = ez + mk * (fd - ez)
            fd_buf[cells, :] = fd + (2.0 * mk) * (ez - fd)
            e_buf[0, x, 0:cy, :] = ex
            e_buf[1, x, 0:cy, :] = ey
            e_buf[2, x, 0:cy, :] = ez
            if t + 1 < STEPS:
                syt[t + 1, 0, pl.ds(x, 1), :] = ex[cy - 1 : cy]
                syt[t + 1, 1, pl.ds(x, 1), :] = ey[cy - 1 : cy]
                syt[t + 1, 2, pl.ds(x, 1), :] = ez[cy - 1 : cy]
                syh[t + 1, 0, pl.ds(x, 1), :] = ex[0:1]
                syh[t + 1, 1, pl.ds(x, 1), :] = ez[0:1]
            return carry

        lax.fori_loop(0, cx, e_plane, 0)
        sent(y_now)
        if t + 1 < STEPS:
            stage_corners(t + 1)
            y_now = y_copies(t + 1)
            begin(y_now)
            x_now = x_copies(t + 1, e_buf.at[:, cx - 1, 0:cy], e_buf.at[1:3, 0, 0:cy])
            begin(x_now)
        first = start[0, 0]
        s_all[t, gy] = row_mask * (
            e_buf[2, 0, pl.ds(first, SY), :] + h_buf[1, 1, pl.ds(PAD + first, SY), :]
        )
        to_peers(lambda peer, t=t: s_all.at[t, gy], s_all.at[t, gy], s_send.at[t], s_recv.at[t])

    stores = [
        pltpu.make_async_copy(e_buf.at[:, 0:cx, 0:cy], fields_out.at[0:3], out_sem.at[0]),
        pltpu.make_async_copy(h_buf.at[:, 1 : cx + 1, PAD : PAD + cy], fields_out.at[3:6], out_sem.at[1]),
    ]
    for store in stores:
        store.start()

    for holder in range(n_y):
        for slot in range(slots):
            cell = target[holder, slot]
            line = fd_buf[pl.ds(jnp.maximum(cell, 0), 1), :]
            alive = jnp.broadcast_to(cell, (1, nz)) >= 0
            fback[holder, slot : slot + 1, :] = jnp.where(alive, line, fin[holder, slot : slot + 1, :])
    to_peers(lambda peer: fback.at[peer], fhome.at[gy], f_send.at[1], f_recv.at[1])
    fhome[gy] = fback[gy]

    for t in range(STEPS):
        wait_all(s_all.at[t], s_recv.at[t])
        q = jnp.dot(s_all[t].reshape(row_count, nz), table[...], precision=HIGH, preferred_element_type=jnp.float32)
        q_real, q_imag = q[:, 0:local_a], q[:, local_a : 2 * local_a]
        g_all[gy, t : t + 1, :] = jnp.sum(q_real * yc[...] - q_imag * ys[...], axis=0, keepdims=True)
        g_all[gy, STEPS + t : STEPS + t + 1, :] = jnp.sum(q_real * ys[...] + q_imag * yc[...], axis=0, keepdims=True)
    to_peers(lambda peer: g_all.at[gy], g_all.at[gy], g_send, g_recv)
    wait_all(fhome, f_recv.at[1])
    home = pltpu.make_async_copy(fhome, fine_out, out_sem.at[2])
    home.start()
    wait_all(g_all, g_recv)
    weights = w_buf[:, 0 : 2 * STEPS]
    for part in range(n_y):
        far_buf[:, part * local_a : (part + 1) * local_a] = jnp.dot(
            weights, g_all[part], precision=HIGH, preferred_element_type=jnp.float32
        )
    far = pltpu.make_async_copy(far_buf, far_out, out_sem.at[3])
    far.start()

    wait_all(fin, f_send.at[0])
    wait_all(fhome, f_send.at[1])
    for t in range(STEPS + 1):
        wait_all(s_all.at[t], s_send.at[t])
    wait_all(g_all, g_send)
    for store in stores:
        store.wait()
    home.wait()
    far.wait()


def shards(
    n_x, n_y, fields, material, ca_table, cb_table, fine, face_target, surf_start, surf_count, omega, bearing
):
    _, cx, cy, nz = fields.shape
    slots = fine.shape[3]
    freqs, angles = omega.shape[0], bearing.shape[0]
    local_a = angles // n_y
    wide = -(-n_y * slots // 128) * 128
    f32 = jnp.float32
    vmem = lambda *shape: pltpu.VMEM(shape, f32)
    dma = pltpu.SemaphoreType.DMA
    any_space = pl.BlockSpec(memory_space=pl.ANY)
    smem = pl.BlockSpec(memory_space=pltpu.SMEM)
    scratch = [
        vmem(3, cx + 1, cy + PAD, nz),
        vmem(3, cx + 1, cy + PAD, nz),
        vmem(cx, cy, nz),
        vmem(cx, cy, nz),
        vmem(cx * cy, nz),
        vmem(cx * cy, nz),
        pltpu.VMEM((cx, cy, nz), jnp.int32),
        vmem(STEPS, 3, cy, nz),
        vmem(STEPS, 2, cy, nz),
        vmem(STEPS, 3, cx, nz),
        vmem(STEPS, 2, cx, nz),
        vmem(STEPS, 8, nz),
        vmem(STEPS, 8, nz),
        vmem(2, cy, nz),
        vmem(2, cx, nz),
        vmem(STEPS, 3, cx, nz),
        vmem(STEPS, 2, cx, nz),
        vmem(2, cx, nz),
        vmem(STEPS, 8, nz),
        vmem(STEPS, 8, nz),
        vmem(STEPS + 1, n_y, SY, nz),
        vmem(n_y, slots, nz),
        vmem(wide, nz),
        vmem(n_y, slots, nz),
        vmem(n_y, slots, nz),
        vmem(nz, 2 * local_a),
        vmem(n_y * SY, local_a),
        vmem(n_y * SY, local_a),
        vmem(2 * freqs, 128),
        vmem(n_y, 2 * STEPS, local_a),
        vmem(2 * freqs, angles),
        dma((4,)),
        dma((6 * STEPS + 2,)),
        dma((6 * STEPS + 2,)),
        dma((STEPS + 1,)),
        dma((STEPS + 1,)),
        dma((2,)),
        dma((2,)),
        dma(()),
        dma(()),
        dma((4,)),
    ]
    out, fine_new, far = pl.pallas_call(
        functools.partial(kernel, n_x, n_y),
        out_shape=(
            jax.ShapeDtypeStruct(fields.shape, f32),
            jax.ShapeDtypeStruct((n_y, slots, nz), f32),
            jax.ShapeDtypeStruct((2 * freqs, angles), f32),
        ),
        in_specs=[any_space] * 3 + [pl.BlockSpec(memory_space=pltpu.VMEM)] + [smem] * 6,
        out_specs=(any_space,) * 3,
        scratch_shapes=scratch,
        compiler_params=pltpu.CompilerParams(
            collective_id=0, has_side_effects=True, vmem_limit_bytes=40 * 1024 * 1024
        ),
    )(
        fields, material, fine.reshape(n_y, slots, nz), bearing.reshape(1, angles),
        ca_table, cb_table, face_target.reshape(n_y, slots), surf_start, surf_count, omega,
    )
    return out, fine_new.reshape(fine.shape), far.reshape(1, 2, freqs, angles)


def solution(mesh):
    in_specs = (
        P(None, "gx", "gy", None),
        P("gx", "gy", None),
        P(),
        P(),
        P("gx", "gy", None, None, None),
        P("gx", "gy", None, None),
        P("gx", "gy"),
        P("gx", "gy"),
        P(),
        P(),
    )
    out_specs = (
        P(None, "gx", "gy", None),
        P("gx", "gy", None, None, None),
        P("gx", None, None, None),
    )
    body = functools.partial(shards, mesh.shape["gx"], mesh.shape["gy"])
    return jax.shard_map(body, mesh=mesh, in_specs=in_specs, out_specs=out_specs, check_vma=False)
```

```python
import functools
import math

import jax
import jax.numpy as jnp
from jax import lax
from jax.experimental import pallas as pl
from jax.experimental.pallas import tpu as pltpu
from jax.sharding import PartitionSpec as P

STEPS = 4
SY = 8
DTH = 0.5
KAPPA = 0.25
WAVENUM = 0.35
PAD = 8

MESH = pl.DeviceIdType.MESH
HIGH = lax.Precision.HIGHEST


def iota(shape, dim):
    return lax.broadcasted_iota(jnp.int32, shape, dim)


def rows_up(value, last):
    count = value.shape[0]
    return jnp.where(iota(value.shape, 0) == count - 1, last, pltpu.roll(value, count - 1, 0))


def z_up(value):
    count = value.shape[1]
    return jnp.where(iota(value.shape, 1) == count - 1, 0.0, pltpu.roll(value, count - 1, 1))


def z_down(value):
    return jnp.where(iota(value.shape, 1) == 0, 0.0, pltpu.roll(value, 1, 1))


def kernel(
    n_x, n_y,
    fields, material, fine, bearing_in, ca_in, cb_in, target_in, start_in, count_in, omega_in,
    fields_out, fine_out, far_out,
    e_buf, h_buf, ca_buf, cb_buf, fd_buf, mk_buf, mat,
    xt, xh, yt, yh, c1, c2, gx_in, gy_in,
    syt, syh, sgy, sc1, sc2,
    s_all, fin, fpad, fback, fhome, table, yc, ys, w_buf, g_all, hrow,
    bearing, ca_table, cb_table, target, start, count, omega,
    load_sem, send_sem, recv_sem, s_send, s_recv, f_send, f_recv, g_send, g_recv, small_sem,
):
    _, cx, cy, nz = fields.shape
    slots = fine.shape[1]
    local_a = g_all.shape[2]
    freqs = omega.shape[0]
    gx = lax.axis_index("gx")
    gy = lax.axis_index("gy")
    has_l, has_r = gx > 0, gx < n_x - 1
    has_d, has_u = gy > 0, gy < n_y - 1
    left, right = (gx - 1, gy), (gx + 1, gy)
    down, up = (gx, gy - 1), (gx, gy + 1)
    left_up, right_down = (gx - 1, gy + 1), (gx + 1, gy - 1)
    has_lu, has_rd = has_l & has_u, has_r & has_d

    loads = [
        pltpu.make_async_copy(fields.at[0:3], e_buf.at[:, 0:cx, 0:cy], load_sem.at[0]),
        pltpu.make_async_copy(fields.at[3:6], h_buf.at[:, 1 : cx + 1, PAD : PAD + cy], load_sem.at[1]),
        pltpu.make_async_copy(material, mat, load_sem.at[2]),
        pltpu.make_async_copy(fine.at[gy], fin.at[gy], load_sem.at[3]),
    ]
    small = [
        pltpu.make_async_copy(src, dst, small_sem.at[index])
        for index, (src, dst) in enumerate((
            (bearing_in, bearing), (ca_in, ca_table), (cb_in, cb_table), (target_in, target),
            (start_in, start), (count_in, count), (omega_in, omega),
        ))
    ]
    for load in loads + small:
        load.start()
    e_buf[:, 0:cx, cy : cy + PAD, :] = jnp.zeros((3, cx, PAD, nz), jnp.float32)

    barrier = pltpu.get_barrier_semaphore()
    for has, where in ((has_l, left), (has_r, right), (has_lu, left_up), (has_rd, right_down)):

        @pl.when(has)
        def _(where=where):
            pl.semaphore_signal(barrier, inc=1, device_id=where, device_id_type=MESH)

    def peer_of(k):
        return lax.rem(gy + k, n_y)

    def greet(k, carry):
        pl.semaphore_signal(barrier, inc=1, device_id=(gx, peer_of(k)), device_id_type=MESH)
        return carry

    lax.fori_loop(1, n_y, greet, 0)

    for has, refs in (
        (has_l, (xt, gx_in)), (has_r, (xh,)), (has_d, (yt, gy_in)), (has_u, (yh,)), (has_lu, (c1,)), (has_rd, (c2,)),
    ):

        @pl.when(jnp.logical_not(has))
        def _(refs=refs):
            for ref in refs:
                ref[...] = jnp.zeros(ref.shape, ref.dtype)

    for load in small:
        load.wait()
    s_all[STEPS, gy] = jnp.broadcast_to(start[0, 0].astype(jnp.float32), (SY, nz))
    arrivals = (
        has_l.astype(jnp.int32) + has_r.astype(jnp.int32) + has_lu.astype(jnp.int32) + has_rd.astype(jnp.int32)
    )
    pl.semaphore_wait(barrier, arrivals + (n_y - 1))

    def remote(index, src, dst, where):
        return pltpu.make_async_remote_copy(
            src_ref=src, dst_ref=dst, send_sem=send_sem.at[index], recv_sem=recv_sem.at[index],
            device_id=where, device_id_type=MESH,
        )

    def x_copies(t, src_tail, src_head):
        return [
            (has_r, has_l, remote(6 * t + 0, src_tail, xt.at[t], right)),
            (has_l, has_r, remote(6 * t + 1, src_head, xh.at[t], left)),
        ]

    def y_copies(t):
        return [
            (has_u, has_d, remote(6 * t + 2, syt.at[t], yt.at[t], up)),
            (has_d, has_u, remote(6 * t + 3, syh.at[t], yh.at[t], down)),
            (has_rd, has_lu, remote(6 * t + 4, sc1.at[t], c1.at[t], right_down)),
            (has_lu, has_rd, remote(6 * t + 5, sc2.at[t], c2.at[t], left_up)),
        ]

    def begin(copies):
        for sends, _, copy in copies:

            @pl.when(sends)
            def _(copy=copy):
                copy.start()

    def arrived(copies):
        for _, comes, copy in copies:

            @pl.when(comes)
            def _(copy=copy):
                copy.wait_recv()

    def sent(copies):
        for sends, _, copy in copies:

            @pl.when(sends)
            def _(copy=copy):
                copy.wait_send()

    def to_peers(src_of, dst, sends, recvs):
        def one(k, carry):
            peer = peer_of(k)
            pltpu.make_async_remote_copy(
                src_ref=src_of(peer), dst_ref=dst, send_sem=sends, recv_sem=recvs,
                device_id=(gx, peer), device_id_type=MESH,
            ).start()
            return carry

        lax.fori_loop(1, n_y, one, 0)

    def wait_all(ref, sem):
        part = ref.at[0 : n_y - 1]
        pltpu.make_async_copy(part, part, sem).wait()

    x_now = x_copies(0, fields.at[0:3, cx - 1], fields.at[1:3, 0])
    x_now.append((has_r, has_l, remote(6 * STEPS, fields.at[4:6, cx - 1], gx_in, right)))
    begin(x_now)
    to_peers(lambda peer: fine.at[peer], fin.at[gy], f_send.at[0], f_recv.at[0])
    to_peers(lambda peer: s_all.at[STEPS, gy], s_all.at[STEPS, gy], s_send.at[STEPS], s_recv.at[STEPS])

    for load in loads[:2]:
        load.wait()

    def stage(x):
        for comp in range(3):
            syt[0, comp, pl.ds(x, 1), :] = e_buf[comp, x, cy - 1 : cy, :]
        syh[0, 0, pl.ds(x, 1), :] = e_buf[0, x, 0:1, :]
        syh[0, 1, pl.ds(x, 1), :] = e_buf[2, x, 0:1, :]
        for part, comp in enumerate((0, 2)):
            line = h_buf[comp, x + 1, PAD + cy - 1 : PAD + cy, :]
            sgy[part, pl.ds(x, 1), :] = line
            hrow[part, pl.ds(x, 1), :] = line

    for x in range(cx):
        stage(x)

    def stage_corners(t):
        sc1[t] = jnp.broadcast_to(e_buf[0, cx - 1, 0:1, :], (8, nz))
        sc2[t] = jnp.broadcast_to(e_buf[1, 0, cy - 1 : cy, :], (8, nz))

    stage_corners(0)
    y_now = y_copies(0)
    y_now.append((has_u, has_d, remote(6 * STEPS + 1, sgy, gy_in, up)))
    begin(y_now)
    own = slice(PAD, PAD + cy)

    def h_plane(x, ey_x, ez_x):
        ex, ey, ez = (e_buf[comp, x, 0:cy, :] for comp in range(3))
        ex_y, ez_y = e_buf[0, x, 1 : cy + 1, :], e_buf[2, x, 1 : cy + 1, :]
        h_buf[0, x + 1, own, :] = h_buf[0, x + 1, own, :] - DTH * ((ez_y - ez) - (z_up(ey) - ey))
        h_buf[1, x + 1, own, :] = h_buf[1, x + 1, own, :] - DTH * ((z_up(ex) - ex) - (ez_x - ez))
        h_buf[2, x + 1, own, :] = h_buf[2, x + 1, own, :] - DTH * ((ey_x - ey) - (ex_y - ex))

    def planes(first, last, one, most=5):
        group = max(k for k in range(1, most + 1) if (last - first) % k == 0)

        def several(index, carry):
            for k in range(group):
                one(first + index * group + k)
            return carry

        lax.fori_loop(0, (last - first) // group, several, 0)

    def h_inside():
        planes(0, cx - 1, lambda x: h_plane(x, e_buf[1, x + 1, 0:cy, :], e_buf[2, x + 1, 0:cy, :]))

    h_inside()

    for load in loads[2:]:
        load.wait()

    def look_up(x, carry):
        index = mat[x]
        ca = jnp.zeros((cy, nz), jnp.float32)
        cb = jnp.zeros((cy, nz), jnp.float32)
        for m in range(ca_table.shape[0]):
            chosen = index == m
            ca = jnp.where(chosen, ca_table[m], ca)
            cb = jnp.where(chosen, cb_table[m], cb)
        ca_buf[x] = ca
        cb_buf[x] = cb
        return carry

    lax.fori_loop(0, cx, look_up, 0)

    angle = bearing[:, pl.ds(pl.multiple_of(gy * local_a, local_a), local_a)]
    cos_b, sin_b = jnp.cos(angle), jnp.sin(angle)
    arg_low = (WAVENUM * iota((8, local_a), 0).astype(jnp.float32)) * cos_b
    cos_low, sin_low = jnp.cos(arg_low), jnp.sin(arg_low)
    tops = nz // 8
    arg_top = ((WAVENUM * 8) * iota((tops, local_a), 0).astype(jnp.float32)) * cos_b
    cos_top, sin_top = jnp.cos(arg_top), jnp.sin(arg_top)
    for top in range(tops):
        ct, st = cos_top[top : top + 1], sin_top[top : top + 1]
        table[8 * top : 8 * top + 8, 0:local_a] = ct * cos_low - st * sin_low
        table[8 * top : 8 * top + 8, local_a : 2 * local_a] = st * cos_low + ct * sin_low

    wait_all(fin, f_recv.at[0])
    fpad[...] = jnp.zeros(fpad.shape, jnp.float32)
    wide = fpad.shape[0]
    lane = iota((1, wide), 1)
    cell_row = jnp.full((1, wide), -1, jnp.int32)
    for holder in range(n_y):
        fpad[slots * holder : slots * (holder + 1), :] = fin[holder]
        for slot in range(slots):
            cell_row = jnp.where(lane == slots * holder + slot, target[slot, holder], cell_row)
    onehot = (iota((cx * cy, wide), 0) == cell_row).astype(jnp.float32).astype(jnp.bfloat16)
    rest = fpad[...]
    dense = jnp.zeros((cx * cy, nz), jnp.float32)
    for _ in range(3):
        part = rest.astype(jnp.bfloat16)
        rest = rest - part.astype(jnp.float32)
        dense = dense + jnp.dot(onehot, part, preferred_element_type=jnp.float32)
    fd_buf[...] = dense
    mk_buf[...] = jnp.dot(
        onehot, jnp.full((wide, nz), KAPPA, jnp.bfloat16), preferred_element_type=jnp.float32
    )

    om = jnp.zeros((freqs, 128), jnp.float32)
    for f in range(freqs):
        om = jnp.where(iota((freqs, 128), 0) == f, omega[f], om)
    lanes = iota((freqs, 128), 1)
    second = lanes >= STEPS
    tick_of = jnp.where(second, lanes - STEPS, lanes) + 1
    moment = om * tick_of.astype(jnp.float32)
    norm = 1.0 / math.sqrt(n_y * SY * nz)
    cos_m, sin_m = jnp.cos(moment) * norm, jnp.sin(moment) * norm
    w_buf[0:freqs, :] = jnp.where(second, sin_m, cos_m)
    w_buf[freqs : 2 * freqs, :] = jnp.where(second, cos_m, -sin_m)

    wait_all(s_all.at[STEPS], s_recv.at[STEPS])
    row_count = n_y * SY
    row = iota((row_count, nz), 0)
    spot = s_all[STEPS].reshape(row_count, nz) + ((row // SY) * cy + lax.rem(row, SY)).astype(jnp.float32)
    arg_y = (WAVENUM * spot[:, 0:1]) * sin_b
    yc[...] = jnp.cos(arg_y)
    ys[...] = jnp.sin(arg_y)

    keep_l = has_l.astype(jnp.float32)
    keep_d = has_d.astype(jnp.float32)
    row_mask = (iota((SY, nz), 0) < count[0, 0]).astype(jnp.float32)

    def far_tick(t):
        wait_all(s_all.at[t], s_recv.at[t])
        q = jnp.dot(s_all[t].reshape(row_count, nz), table[...], precision=HIGH, preferred_element_type=jnp.float32)
        q_real, q_imag = q[:, 0:local_a], q[:, local_a : 2 * local_a]
        g_all[gy, t : t + 1, :] = jnp.sum(q_real * yc[...] - q_imag * ys[...], axis=0, keepdims=True)
        g_all[gy, STEPS + t : STEPS + t + 1, :] = jnp.sum(q_real * ys[...] + q_imag * yc[...], axis=0, keepdims=True)

    def send_surface(t):
        to_peers(lambda peer: s_all.at[t, gy], s_all.at[t, gy], s_send.at[t], s_recv.at[t])

    def keep_surface(t, e_ref):
        first = start[0, 0]
        s_all[t, gy] = row_mask * (
            e_ref[2, 0, pl.ds(first, SY), :] + h_buf[1, 1, pl.ds(PAD + first, SY), :]
        )

    for t in range(STEPS):
        final = t + 1 == STEPS
        if t > 0:
            h_inside()
            send_surface(t - 1)
        if t > 1:
            far_tick(t - 2)
        arrived(x_now)
        arrived(y_now)
        sent(x_now)
        if t == 0:
            h_buf[1, 0, own, :] = gx_in[0]
            h_buf[2, 0, own, :] = gx_in[1]
        h_plane(cx - 1, xh[t, 0], xh[t, 1])
        ex, ey, ez = xt[t, 0], xt[t, 1], xt[t, 2]
        ahead = rows_up(ex, c1[t, 0:1, :])
        h_buf[1, 0, own, :] = keep_l * (
            h_buf[1, 0, own, :] - DTH * ((z_up(ex) - ex) - (e_buf[2, 0, 0:cy, :] - ez))
        )
        h_buf[2, 0, own, :] = keep_l * (
            h_buf[2, 0, own, :] - DTH * ((e_buf[1, 0, 0:cy, :] - ey) - (ahead - ex))
        )
        ex, ey, ez = yt[t, 0], yt[t, 1], yt[t, 2]
        ahead = rows_up(ey, c2[t, 0:1, :])
        gy_in[0] = keep_d * (gy_in[0] - DTH * ((syh[t, 1] - ez) - (z_up(ey) - ey)))
        gy_in[1] = keep_d * (gy_in[1] - DTH * ((ahead - ey) - (syh[t, 0] - ex)))
        ex, ey, ez = syt[t, 0], syt[t, 1], syt[t, 2]
        ahead = rows_up(ey, xh[t, 0, cy - 1 : cy, :])
        hrow[0] = hrow[0] - DTH * ((yh[t, 1] - ez) - (z_up(ey) - ey))
        hrow[1] = hrow[1] - DTH * ((ahead - ey) - (yh[t, 0] - ex))
        for x in range(cx):
            for part, comp in enumerate((0, 2)):
                h_buf[comp, x + 1, PAD - 1 : PAD, :] = gy_in[part, x : x + 1, :]
                h_buf[comp, x + 1, PAD + cy - 1 : PAD + cy, :] = hrow[part, x : x + 1, :]

        def e_plane(x, t=t, final=final):
            before = slice(PAD - 1, PAD + cy - 1)
            hx, hy, hz = (h_buf[comp, x + 1, own, :] for comp in range(3))
            hx_y, hz_y = h_buf[0, x + 1, before, :], h_buf[2, x + 1, before, :]
            hy_x, hz_x = h_buf[1, x, own, :], h_buf[2, x, own, :]
            ca, cb = ca_buf[x], cb_buf[x]
            ex = ca * e_buf[0, x, 0:cy, :] + cb * ((hz - hz_y) - (hy - z_down(hy)))
            ey = ca * e_buf[1, x, 0:cy, :] + cb * ((hx - z_down(hx)) - (hz - hz_x))
            ez = ca * e_buf[2, x, 0:cy, :] + cb * ((hy - hy_x) - (hx - hx_y))
            cells = pl.ds(pl.multiple_of(x * cy, cy), cy)
            mk, fd = mk_buf[cells, :], fd_buf[cells, :]
            ez = ez + mk * (fd - ez)
            fd_buf[cells, :] = fd + (2.0 * mk) * (ez - fd)
            if final:
                for comp, value in enumerate((ex, ey, ez, hx, hy, hz)):
                    fields_out[comp, x] = value
                return
            e_buf[0, x, 0:cy, :] = ex
            e_buf[1, x, 0:cy, :] = ey
            e_buf[2, x, 0:cy, :] = ez
            syt[t + 1, 0, pl.ds(x, 1), :] = ex[cy - 1 : cy]
            syt[t + 1, 1, pl.ds(x, 1), :] = ey[cy - 1 : cy]
            syt[t + 1, 2, pl.ds(x, 1), :] = ez[cy - 1 : cy]
            syh[t + 1, 0, pl.ds(x, 1), :] = ex[0:1]
            syh[t + 1, 1, pl.ds(x, 1), :] = ez[0:1]

        if final:
            e_plane(0)
            keep_surface(t, fields_out)
            send_surface(t)
            planes(1, cx, e_plane)
            sent(y_now)
        else:
            planes(0, cx, e_plane)
            stage_corners(t + 1)
            sent(y_now)
            y_now = y_copies(t + 1)
            begin(y_now)
            x_now = x_copies(t + 1, e_buf.at[:, cx - 1, 0:cy], e_buf.at[1:3, 0, 0:cy])
            begin(x_now)
            keep_surface(t, e_buf)

    for holder in range(n_y):
        for slot in range(slots):
            cell = target[slot, holder]
            line = fd_buf[pl.ds(jnp.maximum(cell, 0), 1), :]
            alive = jnp.broadcast_to(cell, (1, nz)) >= 0
            fback[holder, slot : slot + 1, :] = jnp.where(alive, line, fin[holder, slot : slot + 1, :])
    to_peers(lambda peer: fback.at[peer], fhome.at[gy], f_send.at[1], f_recv.at[1])
    fhome[gy] = fback[gy]

    for t in range(max(0, STEPS - 2), STEPS):
        far_tick(t)
    to_peers(lambda peer: g_all.at[gy], g_all.at[gy], g_send, g_recv)
    wait_all(fhome, f_recv.at[1])
    fine_out[...] = fhome[...]
    wait_all(g_all, g_recv)
    weights = w_buf[:, 0 : 2 * STEPS]
    for part in range(n_y):
        far_out[:, part * local_a : (part + 1) * local_a] = jnp.dot(
            weights, g_all[part], precision=HIGH, preferred_element_type=jnp.float32
        )

    wait_all(fin, f_send.at[0])
    wait_all(fhome, f_send.at[1])
    for t in range(STEPS + 1):
        wait_all(s_all.at[t], s_send.at[t])
    wait_all(g_all, g_send)


def shards(
    n_x, n_y, fields, material, ca_table, cb_table, fine, face_target, surf_start, surf_count, omega, bearing
):
    _, cx, cy, nz = fields.shape
    slots = fine.shape[3]
    freqs, angles = omega.shape[0], bearing.shape[0]
    local_a = angles // n_y
    wide = -(-n_y * slots // 128) * 128
    f32 = jnp.float32
    vmem = lambda *shape: pltpu.VMEM(shape, f32)
    dma = pltpu.SemaphoreType.DMA
    hbm = pl.BlockSpec(memory_space=pltpu.HBM)
    scratch = [
        vmem(3, cx + 1, cy + PAD, nz),
        vmem(3, cx + 1, cy + PAD, nz),
        vmem(cx, cy, nz),
        vmem(cx, cy, nz),
        vmem(cx * cy, nz),
        vmem(cx * cy, nz),
        pltpu.VMEM((cx, cy, nz), jnp.int32),
        vmem(STEPS, 3, cy, nz),
        vmem(STEPS, 2, cy, nz),
        vmem(STEPS, 3, cx, nz),
        vmem(STEPS, 2, cx, nz),
        vmem(STEPS, 8, nz),
        vmem(STEPS, 8, nz),
        vmem(2, cy, nz),
        vmem(2, cx, nz),
        vmem(STEPS, 3, cx, nz),
        vmem(STEPS, 2, cx, nz),
        vmem(2, cx, nz),
        vmem(STEPS, 8, nz),
        vmem(STEPS, 8, nz),
        vmem(STEPS + 1, n_y, SY, nz),
        vmem(n_y, slots, nz),
        vmem(wide, nz),
        vmem(n_y, slots, nz),
        vmem(n_y, slots, nz),
        vmem(nz, 2 * local_a),
        vmem(n_y * SY, local_a),
        vmem(n_y * SY, local_a),
        vmem(2 * freqs, 128),
        vmem(n_y, 2 * STEPS, local_a),
        vmem(2, cx, nz),
        vmem(1, angles),
        pltpu.SMEM(ca_table.shape, f32),
        pltpu.SMEM(cb_table.shape, f32),
        pltpu.SMEM((slots, n_y), jnp.int32),
        pltpu.SMEM((1, 1), jnp.int32),
        pltpu.SMEM((1, 1), jnp.int32),
        pltpu.SMEM(omega.shape, f32),
        dma((4,)),
        dma((6 * STEPS + 2,)),
        dma((6 * STEPS + 2,)),
        dma((STEPS + 1,)),
        dma((STEPS + 1,)),
        dma((2,)),
        dma((2,)),
        dma(()),
        dma(()),
        dma((7,)),
    ]
    out, fine_new, far = pl.pallas_call(
        functools.partial(kernel, n_x, n_y),
        out_shape=(
            jax.ShapeDtypeStruct(fields.shape, f32),
            jax.ShapeDtypeStruct((n_y, slots, nz), f32),
            jax.ShapeDtypeStruct((2 * freqs, angles), f32),
        ),
        in_specs=[hbm] * 10,
        out_specs=(pl.BlockSpec(memory_space=pltpu.VMEM),) * 3,
        scratch_shapes=scratch,
        compiler_params=pltpu.CompilerParams(
            collective_id=0, has_side_effects=True, vmem_limit_bytes=40 * 1024 * 1024
        ),
    )(
        fields, material, fine.reshape(n_y, slots, nz), bearing.reshape(1, angles),
        ca_table, cb_table, face_target.reshape(n_y, slots).T, surf_start, surf_count, omega,
    )
    return out, fine_new.reshape(fine.shape), far.reshape(1, 2, freqs, angles)


def solution(mesh):
    in_specs = (
        P(None, "gx", "gy", None),
        P("gx", "gy", None),
        P(),
        P(),
        P("gx", "gy", None, None, None),
        P("gx", "gy", None, None),
        P("gx", "gy"),
        P("gx", "gy"),
        P(),
        P(),
    )
    out_specs = (
        P(None, "gx", "gy", None),
        P("gx", "gy", None, None, None),
        P("gx", None, None, None),
    )
    body = functools.partial(shards, mesh.shape["gx"], mesh.shape["gy"])
    return jax.shard_map(body, mesh=mesh, in_specs=in_specs, out_specs=out_specs, check_vma=False)
```

```python
import functools
import math

import jax
import jax.numpy as jnp
from jax import lax
from jax.experimental import pallas as pl
from jax.experimental.pallas import tpu as pltpu
from jax.sharding import PartitionSpec as P

STEPS = 4
SY = 8
DTH = 0.5
KAPPA = 0.25
WAVENUM = 0.35
PAD = 8

MESH = pl.DeviceIdType.MESH
HIGH = lax.Precision.HIGHEST


def iota(shape, dim):
    return lax.broadcasted_iota(jnp.int32, shape, dim)


def rows_up(value, last):
    count = value.shape[0]
    return jnp.where(iota(value.shape, 0) == count - 1, last, pltpu.roll(value, count - 1, 0))


def z_up(value):
    count = value.shape[1]
    return jnp.where(iota(value.shape, 1) == count - 1, 0.0, pltpu.roll(value, count - 1, 1))


def z_down(value):
    return jnp.where(iota(value.shape, 1) == 0, 0.0, pltpu.roll(value, 1, 1))


def kernel(
    n_x, n_y,
    fields, material, fine, bearing_in, ca_in, cb_in, target_in, start_in, count_in, omega_in,
    fields_out, fine_out, far_out,
    e_buf, h_buf, ca_buf, cb_buf, fd_buf, mk_buf, mat,
    xt, xh, yt, yh, c1, c2, gx_in, gy_in,
    syt, syh, sgy, sc1, sc2,
    s_all, fin, fpad, fback, fhome, table, yc, ys, w_buf, g_all, hrow,
    bearing, ca_table, cb_table, target, start, count, omega,
    load_sem, send_sem, recv_sem, s_send, s_recv, f_send, f_recv, g_send, g_recv, small_sem,
):
    _, cx, cy, nz = fields.shape
    slots = fine.shape[1]
    local_a = g_all.shape[2]
    freqs = omega.shape[0]
    gx = lax.axis_index("gx")
    gy = lax.axis_index("gy")
    has_l, has_r = gx > 0, gx < n_x - 1
    has_d, has_u = gy > 0, gy < n_y - 1
    left, right = (gx - 1, gy), (gx + 1, gy)
    down, up = (gx, gy - 1), (gx, gy + 1)
    left_up, right_down = (gx - 1, gy + 1), (gx + 1, gy - 1)
    has_lu, has_rd = has_l & has_u, has_r & has_d

    loads = [
        pltpu.make_async_copy(fields.at[0:3], e_buf.at[:, 0:cx, 0:cy], load_sem.at[0]),
        pltpu.make_async_copy(fields.at[3:6], h_buf.at[:, 1 : cx + 1, PAD : PAD + cy], load_sem.at[1]),
        pltpu.make_async_copy(material, mat, load_sem.at[2]),
        pltpu.make_async_copy(fine.at[gy], fin.at[gy], load_sem.at[3]),
    ]
    small = [
        pltpu.make_async_copy(src, dst, small_sem.at[index])
        for index, (src, dst) in enumerate((
            (bearing_in, bearing), (ca_in, ca_table), (cb_in, cb_table), (target_in, target),
            (start_in, start), (count_in, count), (omega_in, omega),
        ))
    ]
    for load in loads + small:
        load.start()
    e_buf[:, 0:cx, cy : cy + PAD, :] = jnp.zeros((3, cx, PAD, nz), jnp.float32)

    barrier = pltpu.get_barrier_semaphore()
    for has, where in ((has_l, left), (has_r, right), (has_lu, left_up), (has_rd, right_down)):

        @pl.when(has)
        def _(where=where):
            pl.semaphore_signal(barrier, inc=1, device_id=where, device_id_type=MESH)

    def peer_of(k):
        return lax.rem(gy + k, n_y)

    def greet(k, carry):
        pl.semaphore_signal(barrier, inc=1, device_id=(gx, peer_of(k)), device_id_type=MESH)
        return carry

    lax.fori_loop(1, n_y, greet, 0)

    for has, refs in (
        (has_l, (xt, gx_in)), (has_r, (xh,)), (has_d, (yt, gy_in)), (has_u, (yh,)), (has_lu, (c1,)), (has_rd, (c2,)),
    ):

        @pl.when(jnp.logical_not(has))
        def _(refs=refs):
            for ref in refs:
                ref[...] = jnp.zeros(ref.shape, ref.dtype)

    for load in small:
        load.wait()
    s_all[STEPS, gy] = jnp.broadcast_to(start[0, 0].astype(jnp.float32), (SY, nz))
    arrivals = (
        has_l.astype(jnp.int32) + has_r.astype(jnp.int32) + has_lu.astype(jnp.int32) + has_rd.astype(jnp.int32)
    )
    pl.semaphore_wait(barrier, arrivals + (n_y - 1))

    def remote(index, src, dst, where):
        return pltpu.make_async_remote_copy(
            src_ref=src, dst_ref=dst, send_sem=send_sem.at[index], recv_sem=recv_sem.at[index],
            device_id=where, device_id_type=MESH,
        )

    def x_copies(t, src_tail, src_head):
        return [
            (has_r, has_l, remote(6 * t + 0, src_tail, xt.at[t], right)),
            (has_l, has_r, remote(6 * t + 1, src_head, xh.at[t], left)),
        ]

    def y_copies(t):
        return [
            (has_u, has_d, remote(6 * t + 2, syt.at[t], yt.at[t], up)),
            (has_d, has_u, remote(6 * t + 3, syh.at[t], yh.at[t], down)),
            (has_rd, has_lu, remote(6 * t + 4, sc1.at[t], c1.at[t], right_down)),
            (has_lu, has_rd, remote(6 * t + 5, sc2.at[t], c2.at[t], left_up)),
        ]

    def begin(copies):
        for sends, _, copy in copies:

            @pl.when(sends)
            def _(copy=copy):
                copy.start()

    def arrived(copies):
        for _, comes, copy in copies:

            @pl.when(comes)
            def _(copy=copy):
                copy.wait_recv()

    def sent(copies):
        for sends, _, copy in copies:

            @pl.when(sends)
            def _(copy=copy):
                copy.wait_send()

    def to_peers(src_of, dst, sends, recvs):
        def one(k, carry):
            peer = peer_of(k)
            pltpu.make_async_remote_copy(
                src_ref=src_of(peer), dst_ref=dst, send_sem=sends, recv_sem=recvs,
                device_id=(gx, peer), device_id_type=MESH,
            ).start()
            return carry

        lax.fori_loop(1, n_y, one, 0)

    def wait_all(ref, sem):
        part = ref.at[0 : n_y - 1]
        pltpu.make_async_copy(part, part, sem).wait()

    x_now = x_copies(0, fields.at[0:3, cx - 1], fields.at[1:3, 0])
    x_now.append((has_r, has_l, remote(6 * STEPS, fields.at[4:6, cx - 1], gx_in, right)))
    begin(x_now)
    to_peers(lambda peer: fine.at[peer], fin.at[gy], f_send.at[0], f_recv.at[0])
    to_peers(lambda peer: s_all.at[STEPS, gy], s_all.at[STEPS, gy], s_send.at[STEPS], s_recv.at[STEPS])

    for load in loads[:2]:
        load.wait()

    def stage(x):
        for comp in range(3):
            syt[0, comp, pl.ds(x, 1), :] = e_buf[comp, x, cy - 1 : cy, :]
        syh[0, 0, pl.ds(x, 1), :] = e_buf[0, x, 0:1, :]
        syh[0, 1, pl.ds(x, 1), :] = e_buf[2, x, 0:1, :]
        for part, comp in enumerate((0, 2)):
            line = h_buf[comp, x + 1, PAD + cy - 1 : PAD + cy, :]
            sgy[part, pl.ds(x, 1), :] = line
            hrow[part, pl.ds(x, 1), :] = line

    for x in range(cx):
        stage(x)

    def stage_corners(t):
        sc1[t] = jnp.broadcast_to(e_buf[0, cx - 1, 0:1, :], (8, nz))
        sc2[t] = jnp.broadcast_to(e_buf[1, 0, cy - 1 : cy, :], (8, nz))

    stage_corners(0)
    y_now = y_copies(0)
    y_now.append((has_u, has_d, remote(6 * STEPS + 1, sgy, gy_in, up)))
    begin(y_now)
    own = slice(PAD, PAD + cy)

    def h_plane(x, ey_x, ez_x):
        ex, ey, ez = (e_buf[comp, x, 0:cy, :] for comp in range(3))
        ex_y, ez_y = e_buf[0, x, 1 : cy + 1, :], e_buf[2, x, 1 : cy + 1, :]
        h_buf[0, x + 1, own, :] = h_buf[0, x + 1, own, :] - DTH * ((ez_y - ez) - (z_up(ey) - ey))
        h_buf[1, x + 1, own, :] = h_buf[1, x + 1, own, :] - DTH * ((z_up(ex) - ex) - (ez_x - ez))
        h_buf[2, x + 1, own, :] = h_buf[2, x + 1, own, :] - DTH * ((ey_x - ey) - (ex_y - ex))

    def planes(first, last, one, most=16):
        group = max(k for k in range(1, most + 1) if (last - first) % k == 0)

        def several(index, carry):
            for k in range(group):
                one(first + index * group + k)
            return carry

        lax.fori_loop(0, (last - first) // group, several, 0)

    def h_inside():
        planes(0, cx - 1, lambda x: h_plane(x, e_buf[1, x + 1, 0:cy, :], e_buf[2, x + 1, 0:cy, :]))

    h_inside()

    for load in loads[2:]:
        load.wait()

    def look_up(x, carry):
        index = mat[x]
        ca = jnp.zeros((cy, nz), jnp.float32)
        cb = jnp.zeros((cy, nz), jnp.float32)
        for m in range(ca_table.shape[0]):
            chosen = index == m
            ca = jnp.where(chosen, ca_table[m], ca)
            cb = jnp.where(chosen, cb_table[m], cb)
        ca_buf[x] = ca
        cb_buf[x] = cb
        return carry

    lax.fori_loop(0, cx, look_up, 0)

    angle = bearing[:, pl.ds(pl.multiple_of(gy * local_a, local_a), local_a)]
    cos_b, sin_b = jnp.cos(angle), jnp.sin(angle)
    arg_low = (WAVENUM * iota((8, local_a), 0).astype(jnp.float32)) * cos_b
    cos_low, sin_low = jnp.cos(arg_low), jnp.sin(arg_low)
    tops = nz // 8
    arg_top = ((WAVENUM * 8) * iota((tops, local_a), 0).astype(jnp.float32)) * cos_b
    cos_top, sin_top = jnp.cos(arg_top), jnp.sin(arg_top)
    for top in range(tops):
        ct, st = cos_top[top : top + 1], sin_top[top : top + 1]
        table[8 * top : 8 * top + 8, 0:local_a] = ct * cos_low - st * sin_low
        table[8 * top : 8 * top + 8, local_a : 2 * local_a] = st * cos_low + ct * sin_low

    wait_all(fin, f_recv.at[0])
    fpad[...] = jnp.zeros(fpad.shape, jnp.float32)
    wide = fpad.shape[0]
    lane = iota((1, wide), 1)
    cell_row = jnp.full((1, wide), -1, jnp.int32)
    for holder in range(n_y):
        fpad[slots * holder : slots * (holder + 1), :] = fin[holder]
        for slot in range(slots):
            cell_row = jnp.where(lane == slots * holder + slot, target[slot, holder], cell_row)
    onehot = (iota((cx * cy, wide), 0) == cell_row).astype(jnp.float32).astype(jnp.bfloat16)
    rest = fpad[...]
    dense = jnp.zeros((cx * cy, nz), jnp.float32)
    for _ in range(3):
        part = rest.astype(jnp.bfloat16)
        rest = rest - part.astype(jnp.float32)
        dense = dense + jnp.dot(onehot, part, preferred_element_type=jnp.float32)
    fd_buf[...] = dense
    mk_buf[...] = jnp.dot(
        onehot, jnp.full((wide, nz), KAPPA, jnp.bfloat16), preferred_element_type=jnp.float32
    )

    om = jnp.zeros((freqs, 128), jnp.float32)
    for f in range(freqs):
        om = jnp.where(iota((freqs, 128), 0) == f, omega[f], om)
    lanes = iota((freqs, 128), 1)
    second = lanes >= STEPS
    tick_of = jnp.where(second, lanes - STEPS, lanes) + 1
    moment = om * tick_of.astype(jnp.float32)
    norm = 1.0 / math.sqrt(n_y * SY * nz)
    cos_m, sin_m = jnp.cos(moment) * norm, jnp.sin(moment) * norm
    w_buf[0:freqs, :] = jnp.where(second, sin_m, cos_m)
    w_buf[freqs : 2 * freqs, :] = jnp.where(second, cos_m, -sin_m)

    wait_all(s_all.at[STEPS], s_recv.at[STEPS])
    row_count = n_y * SY
    row = iota((row_count, nz), 0)
    spot = s_all[STEPS].reshape(row_count, nz) + ((row // SY) * cy + lax.rem(row, SY)).astype(jnp.float32)
    arg_y = (WAVENUM * spot[:, 0:1]) * sin_b
    yc[...] = jnp.cos(arg_y)
    ys[...] = jnp.sin(arg_y)

    keep_l = has_l.astype(jnp.float32)
    keep_d = has_d.astype(jnp.float32)
    row_mask = (iota((SY, nz), 0) < count[0, 0]).astype(jnp.float32)

    def far_tick(t):
        wait_all(s_all.at[t], s_recv.at[t])
        q = jnp.dot(s_all[t].reshape(row_count, nz), table[...], precision=HIGH, preferred_element_type=jnp.float32)
        q_real, q_imag = q[:, 0:local_a], q[:, local_a : 2 * local_a]
        g_all[gy, t : t + 1, :] = jnp.sum(q_real * yc[...] - q_imag * ys[...], axis=0, keepdims=True)
        g_all[gy, STEPS + t : STEPS + t + 1, :] = jnp.sum(q_real * ys[...] + q_imag * yc[...], axis=0, keepdims=True)

    def send_surface(t):
        to_peers(lambda peer: s_all.at[t, gy], s_all.at[t, gy], s_send.at[t], s_recv.at[t])

    def keep_surface(t, e_ref):
        first = start[0, 0]
        s_all[t, gy] = row_mask * (
            e_ref[2, 0, pl.ds(first, SY), :] + h_buf[1, 1, pl.ds(PAD + first, SY), :]
        )

    for t in range(STEPS):
        final = t + 1 == STEPS
        if t > 0:
            h_inside()
            send_surface(t - 1)
        if t > 1:
            far_tick(t - 2)
        arrived(x_now)
        arrived(y_now)
        sent(x_now)
        if t == 0:
            h_buf[1, 0, own, :] = gx_in[0]
            h_buf[2, 0, own, :] = gx_in[1]
        h_plane(cx - 1, xh[t, 0], xh[t, 1])
        ex, ey, ez = xt[t, 0], xt[t, 1], xt[t, 2]
        ahead = rows_up(ex, c1[t, 0:1, :])
        h_buf[1, 0, own, :] = keep_l * (
            h_buf[1, 0, own, :] - DTH * ((z_up(ex) - ex) - (e_buf[2, 0, 0:cy, :] - ez))
        )
        h_buf[2, 0, own, :] = keep_l * (
            h_buf[2, 0, own, :] - DTH * ((e_buf[1, 0, 0:cy, :] - ey) - (ahead - ex))
        )
        ex, ey, ez = yt[t, 0], yt[t, 1], yt[t, 2]
        ahead = rows_up(ey, c2[t, 0:1, :])
        gy_in[0] = keep_d * (gy_in[0] - DTH * ((syh[t, 1] - ez) - (z_up(ey) - ey)))
        gy_in[1] = keep_d * (gy_in[1] - DTH * ((ahead - ey) - (syh[t, 0] - ex)))
        ex, ey, ez = syt[t, 0], syt[t, 1], syt[t, 2]
        ahead = rows_up(ey, xh[t, 0, cy - 1 : cy, :])
        hrow[0] = hrow[0] - DTH * ((yh[t, 1] - ez) - (z_up(ey) - ey))
        hrow[1] = hrow[1] - DTH * ((ahead - ey) - (yh[t, 0] - ex))
        for x in range(cx):
            for part, comp in enumerate((0, 2)):
                h_buf[comp, x + 1, PAD - 1 : PAD, :] = gy_in[part, x : x + 1, :]
                h_buf[comp, x + 1, PAD + cy - 1 : PAD + cy, :] = hrow[part, x : x + 1, :]

        def e_plane(x, t=t, final=final):
            before = slice(PAD - 1, PAD + cy - 1)
            hx, hy, hz = (h_buf[comp, x + 1, own, :] for comp in range(3))
            hx_y, hz_y = h_buf[0, x + 1, before, :], h_buf[2, x + 1, before, :]
            hy_x, hz_x = h_buf[1, x, own, :], h_buf[2, x, own, :]
            ca, cb = ca_buf[x], cb_buf[x]
            ex = ca * e_buf[0, x, 0:cy, :] + cb * ((hz - hz_y) - (hy - z_down(hy)))
            ey = ca * e_buf[1, x, 0:cy, :] + cb * ((hx - z_down(hx)) - (hz - hz_x))
            ez = ca * e_buf[2, x, 0:cy, :] + cb * ((hy - hy_x) - (hx - hx_y))
            cells = pl.ds(pl.multiple_of(x * cy, cy), cy)
            mk, fd = mk_buf[cells, :], fd_buf[cells, :]
            ez = ez + mk * (fd - ez)
            fd_buf[cells, :] = fd + (2.0 * mk) * (ez - fd)
            if final:
                for comp, value in enumerate((ex, ey, ez, hx, hy, hz)):
                    fields_out[comp, x] = value
                return
            e_buf[0, x, 0:cy, :] = ex
            e_buf[1, x, 0:cy, :] = ey
            e_buf[2, x, 0:cy, :] = ez
            syt[t + 1, 0, pl.ds(x, 1), :] = ex[cy - 1 : cy]
            syt[t + 1, 1, pl.ds(x, 1), :] = ey[cy - 1 : cy]
            syt[t + 1, 2, pl.ds(x, 1), :] = ez[cy - 1 : cy]
            syh[t + 1, 0, pl.ds(x, 1), :] = ex[0:1]
            syh[t + 1, 1, pl.ds(x, 1), :] = ez[0:1]

        if final:
            e_plane(0)
            keep_surface(t, fields_out)
            send_surface(t)
            planes(1, cx, e_plane)
            sent(y_now)
        else:
            planes(0, cx, e_plane)
            stage_corners(t + 1)
            sent(y_now)
            y_now = y_copies(t + 1)
            begin(y_now)
            x_now = x_copies(t + 1, e_buf.at[:, cx - 1, 0:cy], e_buf.at[1:3, 0, 0:cy])
            begin(x_now)
            keep_surface(t, e_buf)

    for holder in range(n_y):
        for slot in range(slots):
            cell = target[slot, holder]
            line = fd_buf[pl.ds(jnp.maximum(cell, 0), 1), :]
            alive = jnp.broadcast_to(cell, (1, nz)) >= 0
            fback[holder, slot : slot + 1, :] = jnp.where(alive, line, fin[holder, slot : slot + 1, :])
    to_peers(lambda peer: fback.at[peer], fhome.at[gy], f_send.at[1], f_recv.at[1])
    fhome[gy] = fback[gy]

    for t in range(max(0, STEPS - 2), STEPS):
        far_tick(t)
    to_peers(lambda peer: g_all.at[gy], g_all.at[gy], g_send, g_recv)
    wait_all(fhome, f_recv.at[1])
    fine_out[...] = fhome[...]
    wait_all(g_all, g_recv)
    weights = w_buf[:, 0 : 2 * STEPS]
    for part in range(n_y):
        far_out[:, part * local_a : (part + 1) * local_a] = jnp.dot(
            weights, g_all[part], precision=HIGH, preferred_element_type=jnp.float32
        )

    wait_all(fin, f_send.at[0])
    wait_all(fhome, f_send.at[1])
    for t in range(STEPS + 1):
        wait_all(s_all.at[t], s_send.at[t])
    wait_all(g_all, g_send)


def shards(
    n_x, n_y, fields, material, ca_table, cb_table, fine, face_target, surf_start, surf_count, omega, bearing
):
    _, cx, cy, nz = fields.shape
    slots = fine.shape[3]
    freqs, angles = omega.shape[0], bearing.shape[0]
    local_a = angles // n_y
    wide = -(-n_y * slots // 128) * 128
    f32 = jnp.float32
    vmem = lambda *shape: pltpu.VMEM(shape, f32)
    dma = pltpu.SemaphoreType.DMA
    hbm = pl.BlockSpec(memory_space=pltpu.HBM)
    scratch = [
        vmem(3, cx + 1, cy + PAD, nz),
        vmem(3, cx + 1, cy + PAD, nz),
        vmem(cx, cy, nz),
        vmem(cx, cy, nz),
        vmem(cx * cy, nz),
        vmem(cx * cy, nz),
        pltpu.VMEM((cx, cy, nz), jnp.int32),
        vmem(STEPS, 3, cy, nz),
        vmem(STEPS, 2, cy, nz),
        vmem(STEPS, 3, cx, nz),
        vmem(STEPS, 2, cx, nz),
        vmem(STEPS, 8, nz),
        vmem(STEPS, 8, nz),
        vmem(2, cy, nz),
        vmem(2, cx, nz),
        vmem(STEPS, 3, cx, nz),
        vmem(STEPS, 2, cx, nz),
        vmem(2, cx, nz),
        vmem(STEPS, 8, nz),
        vmem(STEPS, 8, nz),
        vmem(STEPS + 1, n_y, SY, nz),
        vmem(n_y, slots, nz),
        vmem(wide, nz),
        vmem(n_y, slots, nz),
        vmem(n_y, slots, nz),
        vmem(nz, 2 * local_a),
        vmem(n_y * SY, local_a),
        vmem(n_y * SY, local_a),
        vmem(2 * freqs, 128),
        vmem(n_y, 2 * STEPS, local_a),
        vmem(2, cx, nz),
        vmem(1, angles),
        pltpu.SMEM(ca_table.shape, f32),
        pltpu.SMEM(cb_table.shape, f32),
        pltpu.SMEM((slots, n_y), jnp.int32),
        pltpu.SMEM((1, 1), jnp.int32),
        pltpu.SMEM((1, 1), jnp.int32),
        pltpu.SMEM(omega.shape, f32),
        dma((4,)),
        dma((6 * STEPS + 2,)),
        dma((6 * STEPS + 2,)),
        dma((STEPS + 1,)),
        dma((STEPS + 1,)),
        dma((2,)),
        dma((2,)),
        dma(()),
        dma(()),
        dma((7,)),
    ]
    out, fine_new, far = pl.pallas_call(
        functools.partial(kernel, n_x, n_y),
        out_shape=(
            jax.ShapeDtypeStruct(fields.shape, f32),
            jax.ShapeDtypeStruct((n_y, slots, nz), f32),
            jax.ShapeDtypeStruct((2 * freqs, angles), f32),
        ),
        in_specs=[hbm] * 10,
        out_specs=(pl.BlockSpec(memory_space=pltpu.VMEM),) * 3,
        scratch_shapes=scratch,
        compiler_params=pltpu.CompilerParams(
            collective_id=0, has_side_effects=True, vmem_limit_bytes=60 * 1024 * 1024
        ),
    )(
        fields, material, fine.reshape(n_y, slots, nz), bearing.reshape(1, angles),
        ca_table, cb_table, face_target.reshape(n_y, slots).T, surf_start, surf_count, omega,
    )
    def hand_on(a, b, c, a_out, b_out, c_out, sems):
        copies = [pltpu.make_async_copy(p, q, sems.at[k]) for k, (p, q) in enumerate(((a, a_out), (b, b_out), (c, c_out)))]
        for copy in copies:
            copy.start()
        for copy in copies:
            copy.wait()

    out, fine_new, far = pl.pallas_call(
        hand_on,
        out_shape=tuple(jax.ShapeDtypeStruct(v.shape, f32) for v in (out, fine_new, far)),
        in_specs=[pl.BlockSpec(memory_space=pltpu.VMEM)] * 3,
        out_specs=(hbm,) * 3,
        scratch_shapes=[dma((3,))],
    )(out, fine_new, far)
    return out, fine_new.reshape(fine.shape), far.reshape(1, 2, freqs, angles)


def solution(mesh):
    in_specs = (
        P(None, "gx", "gy", None),
        P("gx", "gy", None),
        P(),
        P(),
        P("gx", "gy", None, None, None),
        P("gx", "gy", None, None),
        P("gx", "gy"),
        P("gx", "gy"),
        P(),
        P(),
    )
    out_specs = (
        P(None, "gx", "gy", None),
        P("gx", "gy", None, None, None),
        P("gx", None, None, None),
    )
    body = functools.partial(shards, mesh.shape["gx"], mesh.shape["gy"])
    return jax.shard_map(body, mesh=mesh, in_specs=in_specs, out_specs=out_specs, check_vma=False)
```
